256 devices in a mesh: sec: 64 (over z, x, y_hi), dof: 4 (over y_lo, core).
Axes of the slice: x: 4, y: 4 (y_hi: 2, y_lo: 2; y = y_hi * 2 + y_lo), z: 8, core: 2. Of those that a mesh axis runs over, the one named last changes fastest.
Arguments:
- sector_modes: bfloat16 [128, 32, 32768], P('sec', None, 'dof'), may hold values from -12 to 12
- tip_modes: bfloat16 [128, 64, 128], P('sec'), may hold values from -36 to 36
- tip_index: int32 [128, 128], replicated, may hold values from 0 to 32767
- nominal_eig: float32 [128, 32], P('sec'), may hold values from 0.5 to 2
- measured_eig: float32 [64], replicated, may hold values from 0.5 to 2
- pairing: int32 [64], replicated, may hold values from 0 to 31
Outputs:
- harmonic_modes: bfloat16 [128, 32, 32768], P('sec', None, 'dof')
- mac_values: float32 [128, 32, 64], P('sec')
- normal_matrix: float32 [128, 128], P('sec')
- normal_rhs: float32 [128], P('sec')
The draws below stay inside these ranges and needn't reach their ends.
All inputs are finite; a program needn't handle non-finite values.
Results may differ from the reference program's by a relative error of at most 0.0069.
Values may be sent and summed in bfloat16 or wider, within the bound.
A program may use at most 128 MiB of HBM per device.

```python
import math
import jax
import jax.numpy as jnp
from jax import lax

FAM = 32
MODES = 64
TIPS = 128
SECTORS = 128
DOF = 32768


def draw_sector_modes(key, part):
    key = jax.random.fold_in(key, 11)
    key_base, key_column = jax.random.split(key, 2)
    column = jnp.exp(jax.random.uniform(key_column, (1, 1, DOF), jnp.float32, math.log(0.3), math.log(3.0)))
    base = jnp.clip(jax.random.normal(key_base, (SECTORS, FAM, DOF), jnp.float32), -4.0, 4.0)
    return (base * column).astype(jnp.bfloat16)


def draw_tip_modes(key, part):
    key = jax.random.fold_in(key, 23)
    key_base, key_sector, key_point = jax.random.split(key, 3)
    ramp = jnp.exp(math.log(3.0) * jnp.arange(SECTORS, dtype=jnp.float32) / (SECTORS - 1))
    sector_scale = ramp * jnp.exp(jax.random.uniform(key_sector, (SECTORS,), jnp.float32, math.log(0.5), math.log(1.5)))
    point_scale = jnp.exp(jax.random.uniform(key_point, (TIPS,), jnp.float32, math.log(0.5), math.log(2.0)))
    base = jnp.clip(jax.random.normal(key_base, (SECTORS, MODES, TIPS), jnp.float32), -4.0, 4.0)
    return (base * sector_scale[:, None, None] * point_scale[None, None, :]).astype(jnp.bfloat16)


def touch_ends(result, key, low, high):
    longest = result.shape.index(max(result.shape))
    spots = []
    for shift in (0, 1):
        where = [jax.random.randint(jax.random.fold_in(key, axis), (), 0, length) for axis, length in enumerate(result.shape)]
        where[longest] = (where[longest] + shift) % result.shape[longest]
        spots.append(tuple(where))
    return result.at[spots[0]].set(low).at[spots[1]].set(high)


def steps_of(rng, extent, shards, low, high):
    gain, own = 1.0, jax.random.fold_in(rng, 6)
    for axis_at, blocks in shards:
        draws = jnp.exp(jax.random.uniform(jax.random.fold_in(own, axis_at), (blocks,), jnp.float32, low / len(shards), high / len(shards)))
        gain = gain * jnp.repeat(draws, extent[axis_at] // blocks).reshape([-1 if axis == axis_at else 1 for axis in range(len(extent))])
    return gain


def setup_inputs(seed: int = 0) -> dict:
    arg_keys = jax.random.split(jax.random.key(seed), 7)
    return {
        "sector_modes": draw_sector_modes(jax.random.fold_in(arg_keys[6], 71), 0),
        "tip_modes": draw_tip_modes(jax.random.fold_in(arg_keys[6], 71), 0),
        "tip_index": touch_ends(jax.random.randint(arg_keys[2], (SECTORS, TIPS), 0, DOF), jax.random.fold_in(arg_keys[2], 1), 0, DOF - 1).astype(jnp.int32),
        "nominal_eig": jnp.clip(jnp.exp(math.log(2.0) - 1.3862944 * jax.random.uniform(arg_keys[3], (SECTORS, FAM), jnp.float32) ** steps_of(arg_keys[3], (SECTORS, FAM), ((0, 64),), -0.2, 0.2)), 0.5, 2.0),
        "measured_eig": jnp.clip(jnp.exp(jax.random.uniform(arg_keys[4], (MODES,), jnp.float32, math.log(0.5), math.log(2.0))), 0.5, 2.0),
        "pairing": touch_ends(jax.random.randint(arg_keys[5], (MODES,), 0, FAM), jax.random.fold_in(arg_keys[5], 1), 0, FAM - 1).astype(jnp.int32),
    }


def harmonic_table(row_count, sectors, first_row):
    row_ids = first_row + lax.broadcasted_iota(jnp.int32, (row_count, sectors), 0)
    sector_ids = lax.broadcasted_iota(jnp.int32, (row_count, sectors), 1)
    phase = row_ids * sector_ids % sectors
    angle = phase.astype(jnp.float32) * (2.0 * math.pi / sectors)
    scale = math.sqrt(2.0 / sectors)
    return jnp.where(row_ids <= sectors // 2, jnp.cos(angle), jnp.sin(angle)) * scale

def reference(sector_modes, tip_modes, tip_index, nominal_eig, measured_eig, pairing):
    sectors, families, dof_total = sector_modes.shape
    mode_count = tip_modes.shape[1]
    tip_count = tip_modes.shape[2]
    highest = lax.Precision.HIGHEST
    table = harmonic_table(sectors, sectors, 0)
    table_low = table.astype(jnp.bfloat16)
    harmonic = jnp.einsum('rs,sfd->rfd', table_low.astype(jnp.float32), sector_modes.astype(jnp.float32)).astype(jnp.bfloat16)
    flat_index = tip_index.reshape(-1).astype(jnp.int32)
    samples = jnp.take(harmonic, flat_index, axis=2)
    tips_wide = tip_modes.astype(jnp.float32)

    def project(pieces):
        sample_row, table_row = pieces
        shaped = sample_row.astype(jnp.float32).reshape(families, sectors, tip_count)
        blocks = jnp.einsum('fsp,smp->sfm', shaped, tips_wide)
        projection = jnp.einsum('s,sfm->fm', table_row, blocks, precision=highest)
        weighted = shaped * table_row[None, :, None]
        return (projection, lax.optimization_barrier(jnp.sum(weighted * weighted, axis=(1, 2))))
    projection, mode_power = lax.map(project, (samples, table))
    tip_power = lax.optimization_barrier(jnp.sum(tips_wide * tips_wide, axis=(0, 2)))
    mac_values = sectors * tip_count * projection * projection / ((mode_power[:, :, None] + 1e-06) * (tip_power[None, None, :] + 1e-06))
    family_ids = lax.broadcasted_iota(jnp.int32, (families, mode_count), 0)
    paired = jnp.where(family_ids == pairing[None, :], 4.0, 0.0).astype(jnp.float32)
    weight = mac_values + paired[None, :, :]
    blade_amps = jnp.einsum('rs,rfm->sfm', table, projection, precision=highest)
    target = (measured_eig[None, None, :] - nominal_eig[:, :, None]) * projection
    flat_amps = blade_amps.reshape(sectors, families * mode_count)
    right_term = table[:, :, None] * flat_amps[None, :, :]
    left_term = right_term * weight.reshape(sectors, 1, families * mode_count)
    norm_factor = float(families * mode_count * tip_count)
    normal_matrix = jnp.einsum('rsk,rtk->st', left_term, right_term, precision=highest) / norm_factor
    normal_rhs = jnp.einsum('rsk,rk->s', left_term, target.reshape(sectors, families * mode_count), precision=highest) / norm_factor
    return (harmonic, mac_values, normal_matrix, normal_rhs)
```

```python
import functools
import math

import jax
import jax.numpy as jnp
from jax import lax
from jax.experimental import pallas as pl
from jax.experimental.pallas import tpu as pltpu
from jax.sharding import PartitionSpec as P

MESH = pl.DeviceIdType.MESH


def harmonic_table(row_count, sectors, first_row):
    row_ids = first_row + lax.broadcasted_iota(jnp.int32, (row_count, sectors), 0)
    sector_ids = lax.broadcasted_iota(jnp.int32, (row_count, sectors), 1)
    phase = row_ids * sector_ids % sectors
    angle = phase.astype(jnp.float32) * (2.0 * math.pi / sectors)
    scale = math.sqrt(2.0 / sectors)
    return jnp.where(row_ids <= sectors // 2, jnp.cos(angle), jnp.sin(angle)) * scale


def transform_kernel(n, x_ref, table_ref, out_ref, mid_ref, recv, wide, done, ssem, rsem, lsem):
    me, q = lax.axis_index("sec"), lax.axis_index("dof")
    own = x_ref.shape[0]
    chunks, sectors, rows, lanes = recv.shape

    barrier = pltpu.get_barrier_semaphore()

    def greet(k, c):
        pl.semaphore_signal(barrier, inc=1, device_id=(me ^ k, q), device_id_type=MESH)
        return c

    lax.fori_loop(1, n, greet, 0)
    pl.semaphore_wait(barrier, n - 1)

    def columns(j):
        return pl.ds(pl.multiple_of(lanes * j, lanes), lanes)

    def mine(j):
        return pl.ds(own * j, own)

    for h in range(chunks):
        family = pl.ds(rows * h, rows)

        def send(k, c, h=h, family=family):
            j = me ^ k
            pltpu.make_async_remote_copy(
                src_ref=x_ref.at[:, family, columns(j)],
                dst_ref=recv.at[h, mine(me)],
                send_sem=ssem.at[h],
                recv_sem=rsem.at[h],
                device_id=(j, q),
                device_id_type=MESH,
            ).start()
            return c

        lax.fori_loop(1, n, send, 0)
        pltpu.make_async_copy(x_ref.at[:, family, columns(me)], recv.at[h, mine(me)], lsem.at[h]).start()

    for h in range(chunks):
        family = pl.ds(rows * h, rows)
        others = recv.at[h, pl.ds(0, own * (n - 1))]
        pltpu.make_async_remote_copy(
            src_ref=others, dst_ref=others, send_sem=ssem.at[h], recv_sem=rsem.at[h],
            device_id=(me, q), device_id_type=MESH,
        ).wait_recv()
        pltpu.make_async_copy(recv.at[h, mine(me)], recv.at[h, mine(me)], lsem.at[h]).wait()
        wide[...] = recv[h].reshape(sectors * rows, lanes).astype(jnp.float32)
        table = table_ref[...]
        for f in range(0, rows, 2):
            pair = [wide[pl.ds(f + i, sectors, stride=rows), :] for i in range(2)]
            both = jnp.concatenate(pair, axis=1).astype(jnp.bfloat16)
            result = jnp.dot(table, both, preferred_element_type=jnp.float32)
            for i in range(2):
                done[pl.ds(f + i, sectors, stride=rows), :] = result[:, lanes * i:lanes * (i + 1)]
        mid_ref[h] = done[...].reshape(sectors, rows, lanes).astype(jnp.bfloat16)

        def back(k, c, h=h, family=family):
            j = me ^ k
            pltpu.make_async_remote_copy(
                src_ref=mid_ref.at[h, mine(j)],
                dst_ref=out_ref.at[:, family, columns(me)],
                send_sem=ssem.at[chunks + h],
                recv_sem=rsem.at[chunks + h],
                device_id=(j, q),
                device_id_type=MESH,
            ).start()
            return c

        lax.fori_loop(1, n, back, 0)
        pltpu.make_async_copy(mid_ref.at[h, mine(me)], out_ref.at[:, family, columns(me)], lsem.at[chunks + h]).start()

    for h in range(chunks):
        others = recv.at[h, pl.ds(0, own * (n - 1))]
        first = pltpu.make_async_remote_copy(
            src_ref=others, dst_ref=others, send_sem=ssem.at[h], recv_sem=rsem.at[h],
            device_id=(me, q), device_id_type=MESH,
        )
        first.wait_send()
        target = out_ref.at[:, pl.ds(rows * h, rows), pl.ds(0, lanes * (n - 1))]
        second = pltpu.make_async_remote_copy(
            src_ref=target, dst_ref=target, send_sem=ssem.at[chunks + h], recv_sem=rsem.at[chunks + h],
            device_id=(me, q), device_id_type=MESH,
        )
        second.wait_recv()
        second.wait_send()
        local = out_ref.at[:, pl.ds(rows * h, rows), pl.ds(0, lanes)]
        pltpu.make_async_copy(local, local, lsem.at[chunks + h]).wait()


def transform(sector_modes, table_low, n):
    own, families, dof_local = sector_modes.shape
    sectors = own * n
    lanes = dof_local // n
    chunks = 2
    rows = families // chunks
    vmem = pl.BlockSpec(memory_space=pltpu.VMEM)
    return pl.pallas_call(
        functools.partial(transform_kernel, n),
        out_shape=(
            jax.ShapeDtypeStruct((own, families, dof_local), jnp.bfloat16),
            jax.ShapeDtypeStruct((chunks, sectors, rows, lanes), jnp.bfloat16),
        ),
        in_specs=[vmem, vmem],
        out_specs=(pl.BlockSpec(memory_space=pl.ANY), vmem),
        scratch_shapes=[
            pltpu.VMEM((chunks, sectors, rows, lanes), jnp.bfloat16),
            pltpu.VMEM((sectors * rows, lanes), jnp.float32),
            pltpu.VMEM((sectors * rows, lanes), jnp.float32),
            pltpu.SemaphoreType.DMA((2 * chunks,)),
            pltpu.SemaphoreType.DMA((2 * chunks,)),
            pltpu.SemaphoreType.DMA((2 * chunks,)),
        ],
        compiler_params=pltpu.CompilerParams(
            collective_id=0, has_side_effects=True, vmem_limit_bytes=48 * 2**20
        ),
        name="transform",
    )(sector_modes, table_low)


def on_device(sector_modes, tip_modes, tip_index, nominal_eig, measured_eig, pairing):
    highest = lax.Precision.HIGHEST
    n = lax.axis_size("sec")
    me, q = lax.axis_index("sec"), lax.axis_index("dof")
    local_sectors, families, dof_local = sector_modes.shape
    sectors = local_sectors * n
    mode_count, tip_count = tip_modes.shape[1:]
    lanes = dof_local // n
    table = harmonic_table(sectors, sectors, 0)
    table_mine = harmonic_table(local_sectors, sectors, me * local_sectors)
    harmonic, mid = transform(sector_modes, table.astype(jnp.bfloat16), n)
    mid = mid.transpose(1, 0, 2, 3).reshape(sectors, families, lanes)
    all_tips = lax.all_gather(tip_modes, "sec", axis=0, tiled=True)
    first = q * dof_local + me * lanes
    chosen = tip_index[:, None, :] == first + lax.broadcasted_iota(jnp.int32, (1, lanes, 1), 1)
    chosen = chosen.astype(jnp.bfloat16)
    spread = jnp.einsum("sdp,smp->smd", chosen, all_tips, preferred_element_type=jnp.float32)
    gather = jnp.einsum("rs,smd->rmd", table, spread, precision=highest)
    part = jnp.einsum("rfd,rmd->rfm", mid.astype(jnp.float32), gather, precision=highest)
    counts = jnp.sum(chosen.astype(jnp.float32), axis=2)
    power = jnp.dot(table * table, counts, precision=highest)
    mid_wide = mid.astype(jnp.float32)
    power_part = jnp.einsum("rfd,rd->rf", mid_wide * mid_wide, power, precision=highest)
    both = lax.psum(jnp.concatenate([part, power_part[:, :, None]], axis=2), ("sec", "dof"))
    full = both[:, :, :mode_count]
    projection = lax.dynamic_slice_in_dim(full, me * local_sectors, local_sectors, 0)
    mode_power = lax.dynamic_slice_in_dim(both[:, :, mode_count], me * local_sectors, local_sectors, 0)
    tip_wide = all_tips.astype(jnp.float32)
    tip_power = jnp.sum(tip_wide * tip_wide, axis=(0, 2))
    mac_values = (
        sectors * tip_count * projection * projection
        / ((mode_power[:, :, None] + 1e-06) * (tip_power[None, None, :] + 1e-06))
    )
    family_ids = lax.broadcasted_iota(jnp.int32, (families, mode_count), 0)
    paired = jnp.where(family_ids == pairing[None, :], 4.0, 0.0).astype(jnp.float32)
    weight = mac_values + paired[None, :, :]
    blade_amps = jnp.einsum("rs,rfm->sfm", table, full, precision=highest)
    target = (measured_eig[None, None, :] - nominal_eig[:, :, None]) * projection
    flat_amps = blade_amps.reshape(sectors, families * mode_count)
    right_term = table_mine[:, :, None] * flat_amps[None, :, :]
    left_term = right_term * weight.reshape(local_sectors, 1, families * mode_count)
    norm_factor = float(families * mode_count * tip_count)
    normal_part = jnp.einsum("rsk,rtk->st", left_term, right_term, precision=highest) / norm_factor
    rhs_part = (
        jnp.einsum(
            "rsk,rk->s",
            left_term,
            target.reshape(local_sectors, families * mode_count),
            precision=highest,
        )
        / norm_factor
    )
    normal_matrix, normal_rhs = (
        lax.psum_scatter(normal_part, "sec", scatter_dimension=0, tiled=True),
        lax.psum_scatter(rhs_part, "sec", scatter_dimension=0, tiled=True),
    )
    return (harmonic, mac_values, normal_matrix, normal_rhs)


def solution(mesh):
    return jax.shard_map(
        on_device,
        mesh=mesh,
        in_specs=(P("sec", None, "dof"), P("sec", None, None), P(), P("sec", None), P(), P()),
        out_specs=(P("sec", None, "dof"), P("sec", None, None), P("sec", None), P("sec")),
        check_vma=False,
    )
```

```python
import math

import jax
import jax.numpy as jnp
import numpy as np
from jax import lax
from jax.experimental import pallas as pl
from jax.experimental.pallas import tpu as pltpu
from jax.sharding import PartitionSpec as P

MESH = pl.DeviceIdType.MESH
HIGHEST = lax.Precision.HIGHEST
F32 = jnp.float32
BF16 = jnp.bfloat16
NT = (((1,), (1,)), ((), ()))

SECTORS, FAM, MODES, TIPS, LANES = 128, 32, 64, 128, 128
SEC, DOFS = 64, 4
NZ, NX, NY, NXY = 8, 4, 2, 8
CHUNKS = 2
ROWS = FAM // CHUNKS
HROWS = MODES + 8
QF = FAM // DOFS
STAGES = (
    "in0", "in1", "out0", "out1", "tip_z", "tip_x", "tip_y", "tip_core", "core", "lo",
    "xy", "z", "all_z", "all_xy", "mac", "nz", "nxy", "ndof",
)
STAGE = {name: i for i, name in enumerate(STAGES)}


def tables():
    rows, cols = np.meshgrid(np.arange(SECTORS), np.arange(SECTORS), indexing="ij")
    angle = 2.0 * np.pi * (rows * cols % SECTORS) / SECTORS
    table = math.sqrt(2.0 / SECTORS) * np.where(rows <= SECTORS // 2, np.cos(angle), np.sin(angle))
    table = table.astype(np.float32)

    def split(a):
        high = a.astype(BF16)
        low = (a - high.astype(np.float32)).astype(BF16)
        return np.concatenate([high, low], axis=1)

    xy, z = np.meshgrid(np.arange(NXY), np.arange(NZ), indexing="ij")
    order = (z * NXY + xy).reshape(-1)
    back = np.concatenate([table[2 * order].T, table[2 * order + 1].T], axis=0)
    return table, table.astype(BF16), split(table), split(table * table), back


def body(
    x_ref, tips_ref, index_ref, nominal_ref, measured_ref, pairing_ref,
    table_ref, low_ref, split_ref, square_ref, back_ref,
    out_ref, mac_ref, normal_ref, rhs_ref,
    recv, wide, done, mid, tips, spread, gather, power,
    part, from_core, half, from_lo, mine_xy, from_xy, mine_z, from_z, every, macs,
    n_z, n_from_z, n_xy, n_from_xy, n_dof, ssem, rsem, lsem,
):
    me, q = lax.axis_index("sec"), lax.axis_index("dof")
    z, x, y = me // NXY, (me // NY) % NX, me % NY
    xy = me % NXY
    lo, core = q // 2, q % 2
    quarter = 2 * core + lo

    barrier = pltpu.get_barrier_semaphore()

    def greet(k, c):
        pl.semaphore_signal(barrier, inc=1, device_id=(me ^ k, q), device_id_type=MESH)
        return c

    lax.fori_loop(1, SEC, greet, 0)
    for k in (1, 2, 3):
        pl.semaphore_signal(barrier, inc=1, device_id=(me, q ^ k), device_id_type=MESH)
    pl.semaphore_signal(barrier, inc=1, device_id=(me ^ 1, q ^ 2), device_id_type=MESH)

    def push(stage, src, dst, sec, dof):
        pltpu.make_async_remote_copy(
            src_ref=src, dst_ref=dst, send_sem=ssem.at[STAGE[stage]], recv_sem=rsem.at[STAGE[stage]],
            device_id=(sec, dof), device_id_type=MESH,
        ).start()

    def total(stage, ref):
        return pltpu.make_async_remote_copy(
            src_ref=ref, dst_ref=ref, send_sem=ssem.at[STAGE[stage]], recv_sem=rsem.at[STAGE[stage]],
            device_id=(me, q), device_id_type=MESH,
        )

    sent = []

    def arrived(stage, ref):
        total(stage, ref).wait_recv()
        sent.append((stage, ref))

    def columns(j):
        return pl.ds(pl.multiple_of(LANES * j, LANES), LANES)

    def mine(j):
        return pl.ds(2 * j, 2)

    def send_in(h):
        family = pl.ds(ROWS * h, ROWS)

        def step(k, c):
            j = me ^ k
            push(f"in{h}", x_ref.at[:, family, columns(j)], recv.at[h, mine(me)], j, q)
            return c

        lax.fori_loop(1, SEC, step, 0)
        pltpu.make_async_copy(x_ref.at[:, family, columns(me)], recv.at[h, mine(me)], lsem.at[h]).start()

    def transform(h):
        arrived(f"in{h}", recv.at[h, pl.ds(0, 2 * (SEC - 1))])
        pltpu.make_async_copy(recv.at[h, mine(me)], recv.at[h, mine(me)], lsem.at[h]).wait()
        wide[...] = recv[h].reshape(SECTORS * ROWS, LANES).astype(F32)
        table = low_ref[...]
        for f in range(0, ROWS, 2):
            pair = [wide[pl.ds(f + i, SECTORS, stride=ROWS), :] for i in range(2)]
            both = jnp.concatenate(pair, axis=1).astype(BF16)
            result = jnp.dot(table, both, preferred_element_type=F32)
            for i in range(2):
                done[pl.ds(f + i, SECTORS, stride=ROWS), :] = result[:, LANES * i:LANES * (i + 1)]
        mid[h] = done[...].reshape(SECTORS, ROWS, LANES).astype(BF16)

    def send_out(h):
        family = pl.ds(ROWS * h, ROWS)

        def step(k, c):
            j = me ^ k
            push(f"out{h}", mid.at[h, mine(j)], out_ref.at[:, family, columns(me)], j, q)
            return c

        lax.fori_loop(1, SEC, step, 0)
        pltpu.make_async_copy(mid.at[h, mine(me)], out_ref.at[:, family, columns(me)], lsem.at[CHUNKS + h]).start()

    own_y = pl.ds(2 * y, 2)
    tips[core, z, x, own_y] = tips_ref[:, pl.ds(pl.multiple_of(32 * core, 32), 32), :]
    pl.semaphore_wait(barrier, SEC + 3)
    for k in range(1, NZ):
        push("tip_z", tips.at[core, z, x, own_y], tips.at[core, z, x, own_y], me ^ (NXY * k), q)
    send_in(0)
    arrived("tip_z", tips.at[core, pl.ds(0, NZ - 1), 0, pl.ds(0, 2)])
    for k in range(1, NX):
        push("tip_x", tips.at[core, :, x, own_y], tips.at[core, :, x, own_y], me ^ (NY * k), q)
    send_in(1)
    arrived("tip_x", tips.at[core, :, pl.ds(0, NX - 1), pl.ds(0, 2)])
    push("tip_y", tips.at[core, :, :, own_y], tips.at[core, :, :, own_y], me ^ 1, q ^ 2)
    transform(0)
    send_out(0)
    arrived("tip_y", tips.at[core, :, :, pl.ds(0, 2)])
    push("tip_core", tips.at[core], tips.at[core], me, q ^ 1)
    transform(1)
    send_out(1)
    arrived("tip_core", tips.at[core])

    first = q * (SEC * LANES) + me * LANES
    column_ids = first + lax.broadcasted_iota(jnp.int32, (LANES, TIPS), 0)
    ones = jnp.ones((16, TIPS), BF16)

    def spread_step(s, tip_sum):
        one = [tips[c, s // 16, (s // 4) % 4, s % 4] for c in range(2)]
        block = jnp.concatenate(one + [ones], axis=0)
        chosen = jnp.where(index_ref[pl.ds(s, 1), :] == column_ids, 1.0, 0.0).astype(BF16)
        result = lax.dot_general(block, chosen, NT, preferred_element_type=F32)
        spread[pl.ds(pl.multiple_of(s * HROWS, 8), HROWS), :] = result[:HROWS]
        both = jnp.concatenate(one, axis=0).astype(F32)
        return tip_sum + both * both

    tip_sum = lax.fori_loop(0, SECTORS, spread_step, jnp.zeros((MODES, TIPS), F32), unroll=4)

    def twice(a):
        low = a.astype(BF16)
        return jnp.concatenate([low, low], axis=0)

    for m in range(0, MODES, 2):
        pair = [spread[pl.ds(m + i, SECTORS, stride=HROWS), :] for i in range(2)]
        both = twice(jnp.concatenate(pair, axis=1))
        result = jnp.dot(split_ref[...], both, preferred_element_type=F32)
        for i in range(2):
            gather[pl.ds(m + i, SECTORS, stride=MODES), :] = result[:, LANES * i:LANES * (i + 1)]
    counts = spread[pl.ds(MODES, SECTORS, stride=HROWS), :]
    power[...] = jnp.dot(square_ref[...], twice(counts), preferred_element_type=F32)

    lane_ids = lax.broadcasted_iota(jnp.int32, (FAM, LANES), 1)

    def project_step(j, mode_power):
        cols, squares = [], []
        for l in range(2):
            r = 2 * j + l
            rows = jnp.concatenate([mid[h, r] for h in range(CHUNKS)], axis=0)
            cols.append(rows)
            rows = rows.astype(F32)
            share = jnp.sum(rows * rows * power[pl.ds(r, 1), :], axis=1, keepdims=True)
            mode_power = jnp.where(lane_ids == r, share, mode_power)
        rows = jnp.concatenate(cols, axis=0)
        g = gather[pl.ds(pl.multiple_of(j * LANES, LANES), LANES), :]
        high = g.astype(BF16)
        low = (g - high.astype(F32)).astype(BF16)
        both = lax.dot_general(
            jnp.concatenate([rows, rows], axis=1), jnp.concatenate([high, low], axis=1), NT,
            preferred_element_type=F32,
        )
        pair = jnp.where(lane_ids < MODES, both[:FAM], both[FAM:])
        part[:, (j % NXY) * NZ + j // NXY] = pair.reshape(DOFS, QF, LANES)
        return mode_power

    mode_power = lax.fori_loop(0, SEC, project_step, jnp.zeros((FAM, LANES), F32), unroll=2)
    part[:, SEC] = mode_power.reshape(DOFS, QF, LANES)

    push("core", part.at[pl.ds(2 * (1 - core), 2)], from_core, me, q ^ 1)
    arrived("core", from_core)
    half[...] = part[pl.ds(2 * core, 2)] + from_core[...]
    push("lo", half.at[1 - lo], from_lo, me, q ^ 2)
    arrived("lo", from_lo)
    for i in range(NXY):
        mine_xy[i, pl.ds(0, NZ)] = half[lo, pl.ds(NZ * i, NZ)] + from_lo[pl.ds(NZ * i, NZ)]
        mine_xy[i, NZ] = half[lo, SEC] + from_lo[SEC]

    for k in range(1, NXY):
        push("xy", mine_xy.at[xy ^ k], from_xy.at[xy], me ^ k, q)
    from_xy[xy] = mine_xy[xy]
    arrived("xy", from_xy.at[pl.ds(0, NXY - 1)])
    columns_sum = jnp.sum(from_xy[...], axis=0)
    mine_z[:, 0] = columns_sum[:NZ]
    for i in range(NZ):
        mine_z[i, 1] = columns_sum[NZ]
    for k in range(1, NZ):
        push("z", mine_z.at[z ^ k], from_z.at[z], me ^ (NXY * k), q)
    from_z[z] = mine_z[z]
    arrived("z", from_z.at[pl.ds(0, NZ - 1)])
    whole = jnp.sum(from_z[...], axis=0)
    projection, mode_power = whole[0], whole[1]

    every[xy, z] = projection
    for k in range(1, NZ):
        push("all_z", every.at[xy, z], every.at[xy, z], me ^ (NXY * k), q)

    lane = lax.broadcasted_iota(jnp.int32, (QF, LANES), 1)
    row = lax.broadcasted_iota(jnp.int32, (QF, LANES), 0)

    def by_half(a, b):
        return jnp.where(lane < MODES, a, b)

    own_power = by_half(*[
        jnp.sum(jnp.where(lane == 2 * me + l, mode_power, 0.0), axis=1, keepdims=True) for l in range(2)
    ])
    tip_column = jnp.sum(tip_sum, axis=1, keepdims=True)
    mode_row = lax.broadcasted_iota(jnp.int32, (MODES, LANES), 0)
    mode_lane = lax.broadcasted_iota(jnp.int32, (MODES, LANES), 1) % MODES
    tip_power = jnp.sum(jnp.where(mode_row == mode_lane, tip_column, 0.0), axis=0, keepdims=True)
    mac = (SECTORS * TIPS) * projection * projection / ((own_power + 1e-06) * (tip_power + 1e-06))
    macs[quarter] = mac
    for k in (1, 2, 3):
        push("mac", macs.at[quarter], macs.at[quarter], me, q ^ k)
    family = QF * quarter + row
    pairing = jnp.concatenate([pairing_ref[...]] * 2, axis=1)
    weight = mac + jnp.where(family == pairing, 4.0, 0.0)
    measured = jnp.concatenate([measured_ref[...]] * 2, axis=1)
    nominal_row = lax.broadcasted_iota(jnp.int32, (QF, FAM), 0) + QF * quarter
    nominal_lane = lax.broadcasted_iota(jnp.int32, (QF, FAM), 1)
    nominal = by_half(*[
        jnp.sum(jnp.where(nominal_row == nominal_lane, nominal_ref[pl.ds(l, 1), :], 0.0), axis=1, keepdims=True)
        for l in range(2)
    ])
    pull = weight * ((measured - nominal) * projection)

    arrived("all_z", every.at[0, pl.ds(0, NZ - 1)])
    for k in range(1, NXY):
        push("all_xy", every.at[xy], every.at[xy], me ^ k, q)
    arrived("all_xy", every.at[pl.ds(0, NXY - 1)])

    flat = every.reshape(SEC * QF, LANES)
    amps = []
    for f in range(QF):
        both = jnp.dot(
            back_ref[...], flat[pl.ds(f, SEC, stride=QF), :], precision=HIGHEST, preferred_element_type=F32
        )
        amps.append(both[:SECTORS, :MODES] + both[SECTORS:, MODES:])
    square = lax.broadcasted_iota(jnp.int32, (SECTORS, SECTORS), 0) == lax.broadcasted_iota(
        jnp.int32, (SECTORS, SECTORS), 1
    )
    amps = [jnp.concatenate(amps[f:f + 2], axis=1) for f in range(0, QF, 2)]
    normal = jnp.zeros((SECTORS, SECTORS), F32)
    rhs = jnp.zeros((8, SECTORS), F32)
    for l in range(2):
        table_row = table_ref[pl.ds(2 * me + l, 1), :]
        table_column = jnp.sum(jnp.where(square, table_row, 0.0), axis=1, keepdims=True)
        inner = jnp.zeros((SECTORS, SECTORS), F32)
        inner_rhs = jnp.zeros((8, SECTORS), F32)
        for t in range(QF // 2):
            def flat_row(a, t=t, l=l):
                return jnp.concatenate(
                    [a[2 * t + i:2 * t + i + 1, MODES * l:MODES * (l + 1)] for i in range(2)], axis=1
                )

            a = amps[t]
            inner += lax.dot_general(a * flat_row(weight), a, NT, precision=HIGHEST, preferred_element_type=F32)
            inner_rhs += lax.dot_general(
                jnp.broadcast_to(flat_row(pull), (8, LANES)), a, NT, precision=HIGHEST, preferred_element_type=F32
            )
        normal += inner * table_column * table_row
        rhs += inner_rhs * table_row
    factor = 1.0 / (FAM * MODES * TIPS)
    n_z[:, pl.ds(0, 2)] = (normal * factor).reshape(NZ, 2, 8, SECTORS)
    for i in range(NZ):
        n_z[i, 2] = rhs * factor

    for k in range(1, NZ):
        push("nz", n_z.at[z ^ k], n_from_z.at[z], me ^ (NXY * k), q)
    n_from_z[z] = n_z[z]
    arrived("nz", n_from_z.at[pl.ds(0, NZ - 1)])
    tiles = jnp.sum(n_from_z[...], axis=0)
    for i in range(2):
        n_xy[i, 0] = tiles[i]
        n_xy[i, 1] = tiles[2]
    for k in range(1, NXY):
        push("nxy", n_xy.at[(xy ^ k) // 4], n_from_xy.at[xy], me ^ k, q)
    n_from_xy[xy] = n_xy[xy // 4]
    arrived("nxy", n_from_xy.at[pl.ds(0, NXY - 1)])
    n_dof[q] = jnp.sum(n_from_xy[...], axis=0)
    for k in (1, 2, 3):
        push("ndof", n_dof.at[q], n_dof.at[q], me, q ^ k)
    arrived("ndof", n_dof.at[pl.ds(0, DOFS - 1)])
    tiles = jnp.sum(n_dof[...], axis=0)
    for l in range(2):
        normal_ref[pl.ds(l, 1), :] = jnp.sum(
            jnp.where(row == 2 * (xy % 4) + l, tiles[0], 0.0), axis=0, keepdims=True
        )
    pair_lane = lax.broadcasted_iota(jnp.int32, (1, 2), 1)
    ends = [
        jnp.sum(jnp.where((lane == 2 * me + l) & (row == 0), tiles[1], 0.0), axis=(0, 1), keepdims=True)
        for l in range(2)
    ]
    rhs_ref[...] = jnp.where(pair_lane == 0, ends[0], ends[1])

    arrived("mac", macs.at[pl.ds(0, DOFS - 1)])
    families = macs[...].reshape(FAM, LANES)
    mac_ref[0] = families[:, :MODES]
    mac_ref[1] = families[:, MODES:]

    for h in range(CHUNKS):
        arrived(f"out{h}", out_ref.at[:, pl.ds(ROWS * h, ROWS), pl.ds(0, LANES * (SEC - 1))])
        local = out_ref.at[:, pl.ds(ROWS * h, ROWS), pl.ds(0, LANES)]
        pltpu.make_async_copy(local, local, lsem.at[CHUNKS + h]).wait()
    for stage, ref in sent:
        total(stage, ref).wait_send()


def on_device(sector_modes, tip_modes, tip_index, nominal_eig, measured_eig, pairing):
    table, table_low, table_split, square_split, back = (jnp.asarray(a) for a in tables())
    vmem = pl.BlockSpec(memory_space=pltpu.VMEM)
    tile = (QF, LANES)
    harmonic, mac, normal, rhs = pl.pallas_call(
        body,
        out_shape=(
            jax.ShapeDtypeStruct(sector_modes.shape, BF16),
            jax.ShapeDtypeStruct((2, FAM, MODES), F32),
            jax.ShapeDtypeStruct((2, SECTORS), F32),
            jax.ShapeDtypeStruct((1, 2), F32),
        ),
        in_specs=[vmem] * 11,
        out_specs=(pl.BlockSpec(memory_space=pl.ANY), vmem, vmem, vmem),
        scratch_shapes=[
            pltpu.VMEM((CHUNKS, SECTORS, ROWS, LANES), BF16),
            pltpu.VMEM((SECTORS * ROWS, LANES), F32),
            pltpu.VMEM((SECTORS * ROWS, LANES), F32),
            pltpu.VMEM((CHUNKS, SECTORS, ROWS, LANES), BF16),
            pltpu.VMEM((2, NZ, NX, 2 * NY, MODES // 2, TIPS), BF16),
            pltpu.VMEM((SECTORS * HROWS, LANES), F32),
            pltpu.VMEM((SECTORS * MODES, LANES), F32),
            pltpu.VMEM((SECTORS, LANES), F32),
            pltpu.VMEM((DOFS, SEC + 1) + tile, F32),
            pltpu.VMEM((2, SEC + 1) + tile, F32),
            pltpu.VMEM((2, SEC + 1) + tile, F32),
            pltpu.VMEM((SEC + 1,) + tile, F32),
            pltpu.VMEM((NXY, NZ + 1) + tile, F32),
            pltpu.VMEM((NXY, NZ + 1) + tile, F32),
            pltpu.VMEM((NZ, 2) + tile, F32),
            pltpu.VMEM((NZ, 2) + tile, F32),
            pltpu.VMEM((NXY, NZ) + tile, F32),
            pltpu.VMEM((DOFS,) + tile, F32),
            pltpu.VMEM((NZ, 3, 8, SECTORS), F32),
            pltpu.VMEM((NZ, 3, 8, SECTORS), F32),
            pltpu.VMEM((2, 2, 8, SECTORS), F32),
            pltpu.VMEM((NXY, 2, 8, SECTORS), F32),
            pltpu.VMEM((DOFS, 2, 8, SECTORS), F32),
            pltpu.SemaphoreType.DMA((len(STAGES),)),
            pltpu.SemaphoreType.DMA((len(STAGES),)),
            pltpu.SemaphoreType.DMA((2 * CHUNKS,)),
        ],
        compiler_params=pltpu.CompilerParams(
            collective_id=0, has_side_effects=True, vmem_limit_bytes=48 * 2**20
        ),
        name="identify",
    )(
        sector_modes, tip_modes, tip_index, nominal_eig, measured_eig.reshape(1, MODES),
        pairing.reshape(1, MODES), table, table_low, table_split, square_split, back,
    )
    return harmonic, mac, normal, rhs.reshape(2)


def solution(mesh):
    return jax.shard_map(
        on_device,
        mesh=mesh,
        in_specs=(P("sec", None, "dof"), P("sec", None, None), P(), P("sec", None), P(), P()),
        out_specs=(P("sec", None, "dof"), P("sec", None, None), P("sec", None), P("sec")),
        check_vma=False,
    )
```

```python
import math

import jax
import jax.numpy as jnp
import numpy as np
from jax import lax
from jax.experimental import pallas as pl
from jax.experimental.pallas import tpu as pltpu
from jax.sharding import PartitionSpec as P

MESH = pl.DeviceIdType.MESH
HIGHEST = lax.Precision.HIGHEST
F32 = jnp.float32
BF16 = jnp.bfloat16
NT = (((1,), (1,)), ((), ()))

SECTORS, FAM, MODES, TIPS, LANES = 128, 32, 64, 128, 128
SEC, DOFS = 64, 4
NZ, NX, NY, NXY = 8, 4, 2, 8
CHUNKS = 2
ROWS = FAM // CHUNKS
HROWS = MODES + 8
QF = FAM // DOFS
PAIRS = SEC // 2 + 1
PIECES = 8
STAGES = (
    "in0", "in1", "out0", "out1", "tip_zy", "x1p", "x1m", "x2p", "x2m", "c0", "cm", "cp", "c2",
    "core", "xy", "z", "rows_xy", "rows",
)
STAGE = {name: i for i, name in enumerate(STAGES)}
LOCAL = ("in0", "in1", "out0", "out1", "tips", "index", "nominal", "low", "split", "square", "forth", "back")


def tables():
    rows, cols = np.meshgrid(np.arange(SECTORS), np.arange(SECTORS), indexing="ij")
    angle = 2.0 * np.pi * (rows * cols % SECTORS) / SECTORS
    table = math.sqrt(2.0 / SECTORS) * np.where(rows <= SECTORS // 2, np.cos(angle), np.sin(angle))
    table = table.astype(np.float32)

    def split(a):
        high = a.astype(BF16)
        low = (a - high.astype(np.float32)).astype(BF16)
        return np.concatenate([high, low], axis=1)

    forth = np.concatenate([table[0::2], table[1::2]], axis=0)
    back = np.concatenate([forth.T[0::2], forth.T[1::2]], axis=0)
    return table.astype(BF16), split(table), split(table * table), forth, back


def body(
    x_ref, tips_ref, index_hbm, nominal_hbm, measured_ref, pairing_ref,
    low_hbm, split_hbm, square_hbm, forth_hbm, back_hbm,
    out_ref, mac_ref, normal_ref, rhs_ref,
    index_ref, nominal_ref, low_ref, split_ref, square_ref, forth_ref, back_ref,
    recv, wide, done, mid, tips, spread, gather, gather_split, power, tip_power_ref,
    part, to_core, from_core, half, mine_xy, from_xy, mine_z, from_z, mine_sec, from_sec, mine_rows, from_rows,
    ssem, rsem, lsem,
):
    me, q = lax.axis_index("sec"), lax.axis_index("dof")
    z, x, y = me // NXY, (me // NY) % NX, me % NY
    xy = me % NXY
    lo, core = q // 2, q % 2
    quarter = 2 * core + lo

    barrier = pltpu.get_barrier_semaphore()

    def greet(k, c):
        pl.semaphore_signal(barrier, inc=1, device_id=(me ^ k, q), device_id_type=MESH)
        return c

    lax.fori_loop(1, SEC, greet, 0)
    for k in (1, 2, 3):
        pl.semaphore_signal(barrier, inc=1, device_id=(me, q ^ k), device_id_type=MESH)
    for k in range(1, NXY):
        pl.semaphore_signal(barrier, inc=1, device_id=(me ^ k, q ^ 2), device_id_type=MESH)
        for b in (1, 2, 3):
            pl.semaphore_signal(barrier, inc=1, device_id=(me ^ (NXY * k), q ^ b), device_id_type=MESH)

    def local(name, src, dst):
        return pltpu.make_async_copy(src, dst, lsem.at[LOCAL.index(name)])

    own_y = pl.ds(2 * y, 2)
    half_modes = pl.ds(pl.multiple_of(32 * core, 32), 32)
    own_tips = local("tips", tips_ref.at[:, half_modes, :], tips.at[core, z, x, own_y])
    own_tips.start()
    loads = [
        local(name, src, dst)
        for name, src, dst in (
            ("index", index_hbm, index_ref), ("nominal", nominal_hbm, nominal_ref), ("low", low_hbm, low_ref),
            ("split", split_hbm, split_ref), ("square", square_hbm, square_ref),
            ("forth", forth_hbm, forth_ref), ("back", back_hbm, back_ref),
        )
    ]
    for load in loads:
        load.start()

    def push(stage, src, dst, sec, dof):
        pltpu.make_async_remote_copy(
            src_ref=src, dst_ref=dst, send_sem=ssem.at[STAGE[stage]], recv_sem=rsem.at[STAGE[stage]],
            device_id=(sec, dof), device_id_type=MESH,
        ).start()

    def total(stage, ref):
        return pltpu.make_async_remote_copy(
            src_ref=ref, dst_ref=ref, send_sem=ssem.at[STAGE[stage]], recv_sem=rsem.at[STAGE[stage]],
            device_id=(me, q), device_id_type=MESH,
        )

    sent = []

    def arrived(stage, ref):
        with jax.named_scope("wait_" + stage):
            total(stage, ref).wait_recv()
        sent.append((stage, ref))

    def columns(j):
        return pl.ds(pl.multiple_of(LANES * j, LANES), LANES)

    def mine(j):
        return pl.ds(2 * j, 2)

    def send_in(h):
        family = pl.ds(ROWS * h, ROWS)

        def step(k, c):
            j = me ^ k
            push(f"in{h}", x_ref.at[:, family, columns(j)], recv.at[h, mine(me)], j, q)
            return c

        lax.fori_loop(1, SEC, step, 0)
        local(f"in{h}", x_ref.at[:, family, columns(me)], recv.at[h, mine(me)]).start()

    def transform(h):
        arrived(f"in{h}", recv.at[h, pl.ds(0, 2 * (SEC - 1))])
        local(f"in{h}", recv.at[h, mine(me)], recv.at[h, mine(me)]).wait()
        wide[...] = recv[h].reshape(SECTORS * ROWS, LANES).astype(F32)
        table = low_ref[...]
        for f in range(0, ROWS, 2):
            pair = [wide[pl.ds(f + i, SECTORS, stride=ROWS), :] for i in range(2)]
            both = jnp.concatenate(pair, axis=1).astype(BF16)
            result = jnp.dot(table, both, preferred_element_type=F32)
            for i in range(2):
                done[pl.ds(f + i, SECTORS, stride=ROWS), :] = result[:, LANES * i:LANES * (i + 1)]
        mid[h] = done[...].reshape(SECTORS, ROWS, LANES).astype(BF16)
        family = pl.ds(ROWS * h, ROWS)

        def step(k, c):
            j = me ^ k
            push(f"out{h}", mid.at[h, mine(j)], out_ref.at[:, family, columns(me)], j, q)
            return c

        lax.fori_loop(1, SEC, step, 0)
        local(f"out{h}", mid.at[h, mine(me)], out_ref.at[:, family, columns(me)]).start()

    first = q * (SEC * LANES) + me * LANES
    column_ids = first + lax.broadcasted_iota(jnp.int32, (LANES, TIPS), 0)
    ones = jnp.ones((16, TIPS), BF16)

    def spread_column(at, tip_sum):
        def step(k, tip_sum):
            for i in range(2 * NY):
                s = 2 * NXY * k + 2 * NY * at + i
                one = [tips[c, k, at, i] for c in range(2)]
                block = jnp.concatenate(one + [ones], axis=0)
                chosen = jnp.where(index_ref[pl.ds(s, 1), :] == column_ids, 1.0, 0.0).astype(BF16)
                result = lax.dot_general(block, chosen, NT, preferred_element_type=F32)
                spread[pl.ds(pl.multiple_of(s * HROWS, 8), HROWS), :] = result[:HROWS]
                both = jnp.concatenate(one, axis=0).astype(F32)
                tip_sum = tip_sum + both * both
            return tip_sum

        with jax.named_scope("spread"):
            return lax.fori_loop(0, NZ, step, tip_sum)

    with jax.named_scope("barrier"):
        pl.semaphore_wait(barrier, SEC + 30)
    own_tips.wait()

    own_block = tips.at[core, z, x, own_y]
    for k in range(1, NZ):
        push("tip_zy", own_block, own_block, me ^ (NXY * k), q)
    for k in range(NZ):
        push("tip_zy", own_block, own_block, me ^ (NXY * k + 1), q)
    send_in(0)
    send_in(1)
    for load in loads:
        load.wait()
    arrived("tip_zy", tips.at[core, pl.ds(0, 5), pl.ds(0, 3), pl.ds(0, 2)])
    xp, xm, xf = (x + 1) % NX, (x + 3) % NX, (x + 2) % NX
    right, left = me + NY * (xp - x), me + NY * (xm - x)
    push("x1p", tips.at[core, :, x], tips.at[core, :, x], right, q)
    push("x1m", tips.at[core, :, x], tips.at[core, :, x], left, q)
    push("c0", tips.at[core, :, x], tips.at[core, :, x], me, q ^ 1)
    arrived("c0", tips.at[core, :, x])
    tip_sum = spread_column(x, jnp.zeros((MODES, TIPS), F32))
    arrived("x1p", tips.at[core, :, xm])
    push("x2p", tips.at[core, :, xm, pl.ds(0, 2)], tips.at[core, :, xm, pl.ds(0, 2)], right, q)
    push("cm", tips.at[core, :, xm], tips.at[core, :, xm], me, q ^ 1)
    arrived("x1m", tips.at[core, :, xp])
    push("x2m", tips.at[core, :, xp, pl.ds(2, 2)], tips.at[core, :, xp, pl.ds(2, 2)], left, q)
    push("cp", tips.at[core, :, xp], tips.at[core, :, xp], me, q ^ 1)
    with jax.named_scope("transform0"):
        transform(0)
    arrived("cm", tips.at[core, :, xm])
    tip_sum = spread_column(xm, tip_sum)
    arrived("x2p", tips.at[core, :, xf, pl.ds(0, 2)])
    arrived("x2m", tips.at[core, :, xf, pl.ds(2, 2)])
    push("c2", tips.at[core, :, xf], tips.at[core, :, xf], me, q ^ 1)
    arrived("cp", tips.at[core, :, xp])
    tip_sum = spread_column(xp, tip_sum)
    arrived("c2", tips.at[core, :, xf])
    tip_sum = spread_column(xf, tip_sum)
    with jax.named_scope("transform1"):
        transform(1)

    def twice(a):
        low = a.astype(BF16)
        return jnp.concatenate([low, low], axis=0)

    with jax.named_scope("gather"):
        for m in range(0, MODES, 2):
            pair = [spread[pl.ds(m + i, SECTORS, stride=HROWS), :] for i in range(2)]
            both = twice(jnp.concatenate(pair, axis=1))
            result = jnp.dot(split_ref[...], both, preferred_element_type=F32)
            for i in range(2):
                gather[pl.ds(m + i, SECTORS, stride=MODES), :] = result[:, LANES * i:LANES * (i + 1)]
        counts = spread[pl.ds(MODES, SECTORS, stride=HROWS), :]
        power[...] = jnp.dot(square_ref[...], twice(counts), preferred_element_type=F32)

        def split_step(j, c):
            g = gather[pl.ds(pl.multiple_of(j * LANES, LANES), LANES), :]
            high = g.astype(BF16)
            gather_split[j] = jnp.concatenate([high, (g - high.astype(F32)).astype(BF16)], axis=1)
            return c

        lax.fori_loop(0, SEC, split_step, 0, unroll=2)
        tip_power_ref[...] = jnp.broadcast_to(jnp.sum(tip_sum, axis=1, keepdims=True), (MODES, LANES))


    lane_ids = lax.broadcasted_iota(jnp.int32, (FAM, LANES), 1)

    def project_step(j, mode_power):
        rows = jnp.concatenate([mid[h, 2 * j + l] for l in range(2) for h in range(CHUNKS)], axis=0)
        both = lax.dot_general(
            jnp.concatenate([rows, rows], axis=1), gather_split[j], NT, preferred_element_type=F32
        )
        pair = jnp.where(lane_ids < MODES, both[:FAM], both[FAM:])
        part[:, j] = pair.reshape(DOFS, QF, LANES)
        rows = rows.astype(F32)
        for l in range(2):
            one = rows[FAM * l:FAM * (l + 1)]
            share = jnp.sum(one * one * power[pl.ds(2 * j + l, 1), :], axis=1, keepdims=True)
            mode_power = jnp.where(lane_ids == SEC * l + j, share, mode_power)
        return mode_power

    with jax.named_scope("project"):
        mode_power = lax.fori_loop(0, SEC, project_step, jnp.zeros((FAM, LANES), F32), unroll=4)
        part[:, SEC] = mode_power.reshape(DOFS, QF, LANES)
        part[:, SEC + 1] = jnp.zeros((DOFS, QF, LANES), F32)

    to_core[...] = part[pl.ds(2 * (1 - core), 2)].reshape(2, PAIRS, 2 * QF, LANES).astype(BF16)
    push("core", to_core, from_core, me, q ^ 1)
    arrived("core", from_core)
    sums = part[pl.ds(2 * core, 2)] + from_core[...].astype(F32).reshape(2, 2 * PAIRS, QF, LANES)
    half[...] = sums.reshape(2 * 2 * PAIRS * QF, LANES)

    lane = lax.broadcasted_iota(jnp.int32, (8, LANES), 1)
    row = lax.broadcasted_iota(jnp.int32, (8, LANES), 0)
    family_row = lax.broadcasted_iota(jnp.int32, (QF, FAM), 0)
    family_lane = lax.broadcasted_iota(jnp.int32, (QF, FAM), 1)
    with jax.named_scope("turn"):
        for i in range(2):
            at = 2 * PAIRS * QF * i
            turned = []
            for f in range(QF):
                one = half[pl.ds(at + f, SEC, stride=QF), :].T
                one = jnp.concatenate([one[:MODES], one[MODES:]], axis=1)
                turned.append(one.reshape(NXY, 8, LANES))
            for f in range(0, QF, 2):
                mine_xy[NXY * i:NXY * (i + 1), f // 2] = jnp.concatenate(turned[f:f + 2], axis=1).astype(BF16)
            nominal = jnp.zeros((QF, LANES), F32)
            for l in range(2):
                own = jnp.where(
                    family_row + QF * (2 * core + i) == family_lane, nominal_ref[pl.ds(l, 1), :], 0.0
                )
                own = jnp.sum(own, axis=1, keepdims=True)
                nominal = jnp.where((lane == SEC * l + me) & (lo == i), own, nominal)
            high = nominal.astype(BF16)
            rest = nominal - high.astype(F32)
            middle = rest.astype(BF16)
            last = (rest - middle.astype(F32)).astype(BF16)
            power_tile = half[pl.ds(at + SEC * QF, QF), :].astype(BF16)
            for k in range(NXY):
                mine_xy[NXY * i + k, 4] = jnp.concatenate([power_tile, high], axis=0)
                mine_xy[NXY * i + k, 5] = jnp.concatenate([middle, last], axis=0)
    slot = NXY * lo + xy
    for b in range(2):
        for k in range(1 - b, NXY):
            push("xy", mine_xy.at[NXY * (lo ^ b) + (xy ^ k)], from_xy.at[slot], me ^ k, q ^ (2 * b))
    from_xy[slot] = mine_xy[slot]
    arrived("xy", from_xy.at[pl.ds(0, 2 * NXY - 1)])
    column = jnp.sum(from_xy[...].astype(F32), axis=0)
    families = column[:4].reshape(QF, 8, LANES)
    power_tile, nominal = column[4, :8], column[4, 8:] + column[5, :8] + column[5, 8:]
    mine_z[:, 0] = families
    for i in range(NZ):
        mine_z[i, 1] = power_tile
        mine_z[i, 2] = nominal
    for k in range(1, NZ):
        push("z", mine_z.at[z ^ k], from_z.at[z], me ^ (NXY * k), q)
    from_z[z] = mine_z[z]
    arrived("z", from_z.at[pl.ds(0, NZ - 1)])
    whole = jnp.sum(from_z[...], axis=0)

    with jax.named_scope("normal"):
        projection = whole[0]
        mode_power, nominal = (
            jnp.sum(jnp.where(row == z, whole[i], 0.0), axis=0, keepdims=True) for i in (1, 2)
        )
        tip_power = tip_power_ref[pl.ds(pl.multiple_of(8 * xy, 8), 8), :]
        mac = (SECTORS * TIPS) * projection * projection / ((mode_power + 1e-06) * (tip_power + 1e-06))
        own_mode = lax.broadcasted_iota(jnp.int32, (8, MODES), 1) == 8 * xy + lax.broadcasted_iota(
            jnp.int32, (8, MODES), 0
        )
        pairing = jnp.sum(jnp.where(own_mode, pairing_ref[...].astype(F32), 0.0), axis=1, keepdims=True)
        measured = jnp.sum(jnp.where(own_mode, measured_ref[...], 0.0), axis=1, keepdims=True)
        family = (QF * quarter + z).astype(F32)
        weight = mac + jnp.where(pairing == family, 4.0, 0.0)
        pull = weight * ((measured - nominal) * projection)
        mac_rows = lax.dot_general(
            mac, jnp.where(own_mode, 1.0, 0.0), (((0,), (0,)), ((), ())),
            precision=HIGHEST, preferred_element_type=F32,
        )

        forth, back = forth_ref[...], back_ref[...]
        amps = jnp.dot(projection, forth, precision=HIGHEST, preferred_element_type=F32)
        amps_column = lax.dot_general(back, projection, NT, precision=HIGHEST, preferred_element_type=F32)
        left = jnp.concatenate([back * weight[k:k + 1, :] for k in range(8)], axis=0)
        pairs = jnp.dot(left, forth, precision=HIGHEST, preferred_element_type=F32)
        normal = jnp.zeros((SECTORS, SECTORS), F32)
        for k in range(8):
            normal += amps_column[:, k:k + 1] * (amps[k:k + 1, :] * pairs[SECTORS * k:SECTORS * (k + 1)])
        pulled = jnp.dot(pull, forth, precision=HIGHEST, preferred_element_type=F32)
        rhs = jnp.sum(amps * pulled, axis=0, keepdims=True)
        factor = 1.0 / (FAM * MODES * TIPS)
        normal = normal * factor
        rows = (
            normal[:SEC], normal[SEC:], jnp.broadcast_to(rhs * factor, (SEC, SECTORS)),
            jnp.concatenate([mac_rows[:SEC], mac_rows[SEC:]], axis=1),
        )
        for i in range(4):
            mine_sec[:, :, i, :] = rows[i].reshape(NZ, NXY, SECTORS)

    for k in range(1, NXY):
        push("rows_xy", mine_sec.at[:, xy ^ k], from_sec.at[xy], me ^ k, q)
    from_sec[xy] = mine_sec[:, xy]
    arrived("rows_xy", from_sec.at[pl.ds(0, NXY - 1)])
    mine_rows[...] = jnp.sum(from_sec[...], axis=0)
    slot = NZ * q + z
    for b in range(DOFS):
        for k in range(0 if b else 1, NZ):
            push("rows", mine_rows.at[z ^ k], from_rows.at[slot], me ^ (NXY * k), q ^ b)
    from_rows[slot] = mine_rows[z]
    arrived("rows", from_rows.at[pl.ds(0, DOFS * NZ - 1)])
    rows = jnp.sum(from_rows[...], axis=0)
    normal_ref[...] = rows[:2]
    pair_lane = lax.broadcasted_iota(jnp.int32, (1, 2), 1)
    rhs_lane = lax.broadcasted_iota(jnp.int32, (1, LANES), 1)
    ends = [
        jnp.sum(jnp.where(rhs_lane == 2 * me + l, rows[2:3], 0.0), axis=1, keepdims=True) for l in range(2)
    ]
    rhs_ref[...] = jnp.where(pair_lane == 0, ends[0], ends[1])
    for i in range(DOFS):
        tile = from_rows[NZ * i:NZ * (i + 1), 3, :]
        for l in range(2):
            mac_ref[l, pl.ds(QF * (2 * (i % 2) + i // 2), QF), :] = tile[:, MODES * l:MODES * (l + 1)]

    for h in range(CHUNKS):
        arrived(f"out{h}", out_ref.at[:, pl.ds(ROWS * h, ROWS), pl.ds(0, LANES * (SEC - 1))])
        own = out_ref.at[:, pl.ds(ROWS * h, ROWS), pl.ds(0, LANES)]
        local(f"out{h}", own, own).wait()
    for stage, ref in sent:
        total(stage, ref).wait_send()


def write(long_ref, *refs):
    short, long_out, short_out = refs[:3], refs[3], refs[4:7]
    held, short_sems, in_sems, out_sems = refs[7:]
    count, width = held.shape[0], held.shape[-1]
    parts = [pl.ds(width * i, width) for i in range(count)]
    copies = [pltpu.make_async_copy(long_ref.at[:, :, parts[i]], held.at[i], in_sems.at[i]) for i in range(count)]
    for copy in copies:
        copy.start()
    ends = [pltpu.make_async_copy(short[i], short_out[i], short_sems.at[i]) for i in range(3)]
    for end in ends:
        end.start()
    for i in range(count):
        copies[i].wait()
        end = pltpu.make_async_copy(held.at[i], long_out.at[:, :, parts[i]], out_sems.at[i])
        end.start()
        ends.append(end)
    for end in ends:
        end.wait()


def on_device(sector_modes, tip_modes, tip_index, nominal_eig, measured_eig, pairing):
    constants = [jnp.asarray(a) for a in tables()]
    vmem = pl.BlockSpec(memory_space=pltpu.VMEM)
    hbm = pl.BlockSpec(memory_space=pltpu.HBM)
    tile = (QF, LANES)
    results = pl.pallas_call(
        body,
        out_shape=(
            jax.ShapeDtypeStruct(sector_modes.shape, BF16),
            jax.ShapeDtypeStruct((2, FAM, MODES), F32),
            jax.ShapeDtypeStruct((2, SECTORS), F32),
            jax.ShapeDtypeStruct((1, 2), F32),
        ),
        in_specs=[hbm] * 4 + [vmem] * 2 + [hbm] * 5,
        out_specs=(hbm, vmem, vmem, vmem),
        scratch_shapes=[
            pltpu.VMEM((SECTORS, TIPS), jnp.int32),
            pltpu.VMEM((2, FAM), F32),
            pltpu.VMEM((SECTORS, SECTORS), BF16),
            pltpu.VMEM((SECTORS, 2 * SECTORS), BF16),
            pltpu.VMEM((SECTORS, 2 * SECTORS), BF16),
            pltpu.VMEM((SECTORS, SECTORS), F32),
            pltpu.VMEM((SECTORS, SECTORS), F32),
            pltpu.VMEM((CHUNKS, SECTORS, ROWS, LANES), BF16),
            pltpu.VMEM((SECTORS * ROWS, LANES), F32),
            pltpu.VMEM((SECTORS * ROWS, LANES), F32),
            pltpu.VMEM((CHUNKS, SECTORS, ROWS, LANES), BF16),
            pltpu.VMEM((2, NZ, NX, 2 * NY, MODES // 2, TIPS), BF16),
            pltpu.VMEM((SECTORS * HROWS, LANES), F32),
            pltpu.VMEM((SECTORS * MODES, LANES), F32),
            pltpu.VMEM((SEC, LANES, 2 * LANES), BF16),
            pltpu.VMEM((SECTORS, LANES), F32),
            pltpu.VMEM((MODES, LANES), F32),
            pltpu.VMEM((DOFS, 2 * PAIRS) + tile, F32),
            pltpu.VMEM((2, PAIRS, 2 * QF, LANES), BF16),
            pltpu.VMEM((2, PAIRS, 2 * QF, LANES), BF16),
            pltpu.VMEM((2 * 2 * PAIRS * QF, LANES), F32),
            pltpu.VMEM((2 * NXY, 6, 16, LANES), BF16),
            pltpu.VMEM((2 * NXY, 6, 16, LANES), BF16),
            pltpu.VMEM((NZ, 3) + tile, F32),
            pltpu.VMEM((NZ, 3) + tile, F32),
            pltpu.VMEM((NZ, NXY, 4, LANES), F32),
            pltpu.VMEM((NXY, NZ, 4, LANES), F32),
            pltpu.VMEM((NZ, 4, LANES), F32),
            pltpu.VMEM((DOFS * NZ, 4, LANES), F32),
            pltpu.SemaphoreType.DMA((len(STAGES),)),
            pltpu.SemaphoreType.DMA((len(STAGES),)),
            pltpu.SemaphoreType.DMA((len(LOCAL),)),
        ],
        compiler_params=pltpu.CompilerParams(
            collective_id=0, has_side_effects=True, vmem_limit_bytes=60 * 2**20
        ),
        name="identify",
    )(
        sector_modes, tip_modes, tip_index, nominal_eig, measured_eig.reshape(1, MODES),
        pairing.reshape(1, MODES), *constants,
    )
    harmonic, mac, normal, rhs = pl.pallas_call(
        write,
        out_shape=[jax.ShapeDtypeStruct(a.shape, a.dtype) for a in results],
        in_specs=[hbm] + [vmem] * 3,
        out_specs=[hbm] * 4,
        scratch_shapes=[
            pltpu.VMEM((PIECES, 2, FAM, sector_modes.shape[2] // PIECES), BF16),
            pltpu.SemaphoreType.DMA((3,)),
            pltpu.SemaphoreType.DMA((PIECES,)),
            pltpu.SemaphoreType.DMA((PIECES,)),
        ],
        name="write",
    )(*results)
    return harmonic, mac, normal, rhs.reshape(2)


def solution(mesh):
    return jax.shard_map(
        on_device,
        mesh=mesh,
        in_specs=(P("sec", None, "dof"), P("sec", None, None), P(), P("sec", None), P(), P()),
        out_specs=(P("sec", None, "dof"), P("sec", None, None), P("sec", None), P("sec")),
        check_vma=False,
    )
```

```python
import math

import jax
import jax.numpy as jnp
import numpy as np
from jax import lax
from jax.experimental import pallas as pl
from jax.experimental.pallas import tpu as pltpu
from jax.sharding import PartitionSpec as P

MESH = pl.DeviceIdType.MESH
HIGHEST = lax.Precision.HIGHEST
F32 = jnp.float32
BF16 = jnp.bfloat16
NT = (((1,), (1,)), ((), ()))

SECTORS, FAM, MODES, TIPS, LANES = 128, 32, 64, 128, 128
SEC, DOFS = 64, 4
NZ, NX, NY, NXY = 8, 4, 2, 8
CHUNKS = 2
ROWS = FAM // CHUNKS
HROWS = MODES + 8
QF = FAM // DOFS
PAIRS = SEC // 2 + 1
STAGES = (
    "in0", "in1", "out0", "out1", "tip_zy", "x1p", "x1m", "x2p", "x2m", "c0", "cm", "cp", "c2",
    "core", "xy", "z", "rows_xy", "rows",
)
STAGE = {name: i for i, name in enumerate(STAGES)}
LOCAL = ("in0", "in1", "out0", "out1", "tips", "index", "nominal", "measured", "pairing", "low", "split", "square", "forth", "back")


def tables():
    rows, cols = np.meshgrid(np.arange(SECTORS), np.arange(SECTORS), indexing="ij")
    angle = 2.0 * np.pi * (rows * cols % SECTORS) / SECTORS
    table = math.sqrt(2.0 / SECTORS) * np.where(rows <= SECTORS // 2, np.cos(angle), np.sin(angle))
    table = table.astype(np.float32)

    def split(a):
        high = a.astype(BF16)
        low = (a - high.astype(np.float32)).astype(BF16)
        return np.concatenate([high, low], axis=1)

    forth = np.concatenate([table[0::2], table[1::2]], axis=0)
    back = np.concatenate([forth.T[0::2], forth.T[1::2]], axis=0)
    return table.astype(BF16), split(table), split(table * table), forth, back


def body(
    x_ref, tips_ref, index_hbm, nominal_hbm, measured_hbm, pairing_hbm,
    low_hbm, split_hbm, square_hbm, forth_hbm, back_hbm,
    out_ref, mac_ref, normal_ref, rhs_ref,
    index_ref, nominal_ref, measured_ref, pairing_ref, low_ref, split_ref, square_ref, forth_ref, back_ref,
    recv, wide, done, mid, tips, spread, gather, gather_split, power, tip_power_ref,
    part, to_core, from_core, half, mine_xy, from_xy, mine_z, from_z, mine_sec, from_sec, mine_rows, from_rows,
    ssem, rsem, lsem,
):
    me, q = lax.axis_index("sec"), lax.axis_index("dof")
    z, x, y = me // NXY, (me // NY) % NX, me % NY
    xy = me % NXY
    lo, core = q // 2, q % 2
    quarter = 2 * core + lo

    barrier = pltpu.get_barrier_semaphore()

    def greet(k, c):
        pl.semaphore_signal(barrier, inc=1, device_id=(me ^ k, q), device_id_type=MESH)
        return c

    lax.fori_loop(1, SEC, greet, 0)
    for k in (1, 2, 3):
        pl.semaphore_signal(barrier, inc=1, device_id=(me, q ^ k), device_id_type=MESH)
    for k in range(1, NXY):
        pl.semaphore_signal(barrier, inc=1, device_id=(me ^ k, q ^ 2), device_id_type=MESH)
        for b in (1, 2, 3):
            pl.semaphore_signal(barrier, inc=1, device_id=(me ^ (NXY * k), q ^ b), device_id_type=MESH)

    def local(name, src, dst):
        return pltpu.make_async_copy(src, dst, lsem.at[LOCAL.index(name)])

    own_y = pl.ds(2 * y, 2)
    half_modes = pl.ds(pl.multiple_of(32 * core, 32), 32)
    own_tips = local("tips", tips_ref.at[:, half_modes, :], tips.at[core, z, x, own_y])
    own_tips.start()
    loads = [
        local(name, src, dst)
        for name, src, dst in (
            ("index", index_hbm, index_ref), ("nominal", nominal_hbm, nominal_ref),
            ("measured", measured_hbm, measured_ref), ("pairing", pairing_hbm, pairing_ref), ("low", low_hbm, low_ref),
            ("split", split_hbm, split_ref), ("square", square_hbm, square_ref),
            ("forth", forth_hbm, forth_ref), ("back", back_hbm, back_ref),
        )
    ]
    for load in loads:
        load.start()

    def push(stage, src, dst, sec, dof):
        pltpu.make_async_remote_copy(
            src_ref=src, dst_ref=dst, send_sem=ssem.at[STAGE[stage]], recv_sem=rsem.at[STAGE[stage]],
            device_id=(sec, dof), device_id_type=MESH,
        ).start()

    def total(stage, ref):
        return pltpu.make_async_remote_copy(
            src_ref=ref, dst_ref=ref, send_sem=ssem.at[STAGE[stage]], recv_sem=rsem.at[STAGE[stage]],
            device_id=(me, q), device_id_type=MESH,
        )

    sent = []

    def arrived(stage, ref):
        with jax.named_scope("wait_" + stage):
            total(stage, ref).wait_recv()
        sent.append((stage, ref))

    def columns(j):
        return pl.ds(pl.multiple_of(LANES * j, LANES), LANES)

    def mine(j):
        return pl.ds(2 * j, 2)

    def send_in(h):
        family = pl.ds(ROWS * h, ROWS)

        def step(k, c):
            j = me ^ k
            push(f"in{h}", x_ref.at[:, family, columns(j)], recv.at[h, mine(me)], j, q)
            return c

        lax.fori_loop(1, SEC, step, 0)
        local(f"in{h}", x_ref.at[:, family, columns(me)], recv.at[h, mine(me)]).start()

    def transform(h):
        arrived(f"in{h}", recv.at[h, pl.ds(0, 2 * (SEC - 1))])
        local(f"in{h}", recv.at[h, mine(me)], recv.at[h, mine(me)]).wait()
        wide[...] = recv[h].reshape(SECTORS * ROWS, LANES).astype(F32)
        table = low_ref[...]
        for f in range(0, ROWS, 2):
            pair = [wide[pl.ds(f + i, SECTORS, stride=ROWS), :] for i in range(2)]
            both = jnp.concatenate(pair, axis=1).astype(BF16)
            result = jnp.dot(table, both, preferred_element_type=F32)
            for i in range(2):
                done[pl.ds(f + i, SECTORS, stride=ROWS), :] = result[:, LANES * i:LANES * (i + 1)]
        mid[h] = done[...].reshape(SECTORS, ROWS, LANES).astype(BF16)

    def send_out(h, low, high):
        family = pl.ds(ROWS * h, ROWS)

        def step(k, c):
            j = me ^ k
            push(f"out{h}", mid.at[h, mine(j)], out_ref.at[:, family, columns(me)], j, q)
            return c

        lax.fori_loop(low, high, step, 0)
        if low == 1:
            local(f"out{h}", mid.at[h, mine(me)], out_ref.at[:, family, columns(me)]).start()

    first = q * (SEC * LANES) + me * LANES
    column_ids = first + lax.broadcasted_iota(jnp.int32, (LANES, TIPS), 0)
    ones = jnp.ones((16, TIPS), BF16)

    def spread_column(at, tip_sum):
        def step(k, tip_sum):
            for i in range(2 * NY):
                s = 2 * NXY * k + 2 * NY * at + i
                one = [tips[c, k, at, i] for c in range(2)]
                block = jnp.concatenate(one + [ones], axis=0)
                chosen = jnp.where(index_ref[pl.ds(s, 1), :] == column_ids, 1.0, 0.0).astype(BF16)
                result = lax.dot_general(block, chosen, NT, preferred_element_type=F32)
                spread[pl.ds(pl.multiple_of(s * HROWS, 8), HROWS), :] = result[:HROWS]
                both = jnp.concatenate(one, axis=0).astype(F32)
                tip_sum = tip_sum + both * both
            return tip_sum

        with jax.named_scope("spread"):
            return lax.fori_loop(0, NZ, step, tip_sum)

    with jax.named_scope("barrier"):
        pl.semaphore_wait(barrier, SEC + 30)
    own_tips.wait()

    own_block = tips.at[core, z, x, own_y]
    for k in range(1, NZ):
        push("tip_zy", own_block, own_block, me ^ (NXY * k), q)
    for k in range(NZ):
        push("tip_zy", own_block, own_block, me ^ (NXY * k + 1), q)
    send_in(0)
    send_in(1)
    for load in loads:
        load.wait()
    arrived("tip_zy", tips.at[core, pl.ds(0, 5), pl.ds(0, 3), pl.ds(0, 2)])
    xp, xm, xf = (x + 1) % NX, (x + 3) % NX, (x + 2) % NX
    right, left = me + NY * (xp - x), me + NY * (xm - x)
    push("x1p", tips.at[core, :, x], tips.at[core, :, x], right, q)
    push("x1m", tips.at[core, :, x], tips.at[core, :, x], left, q)
    push("c0", tips.at[core, :, x], tips.at[core, :, x], me, q ^ 1)
    arrived("c0", tips.at[core, :, x])
    tip_sum = spread_column(x, jnp.zeros((MODES, TIPS), F32))
    arrived("x1p", tips.at[core, :, xm])
    push("x2p", tips.at[core, :, xm, pl.ds(0, 2)], tips.at[core, :, xm, pl.ds(0, 2)], right, q)
    push("cm", tips.at[core, :, xm], tips.at[core, :, xm], me, q ^ 1)
    arrived("x1m", tips.at[core, :, xp])
    push("x2m", tips.at[core, :, xp, pl.ds(2, 2)], tips.at[core, :, xp, pl.ds(2, 2)], left, q)
    push("cp", tips.at[core, :, xp], tips.at[core, :, xp], me, q ^ 1)
    with jax.named_scope("transform0"):
        transform(0)
        send_out(0, 1, SEC)
    arrived("cm", tips.at[core, :, xm])
    tip_sum = spread_column(xm, tip_sum)
    arrived("x2p", tips.at[core, :, xf, pl.ds(0, 2)])
    arrived("x2m", tips.at[core, :, xf, pl.ds(2, 2)])
    push("c2", tips.at[core, :, xf], tips.at[core, :, xf], me, q ^ 1)
    arrived("cp", tips.at[core, :, xp])
    tip_sum = spread_column(xp, tip_sum)
    arrived("c2", tips.at[core, :, xf])
    tip_sum = spread_column(xf, tip_sum)

    def twice(a):
        low = a.astype(BF16)
        return jnp.concatenate([low, low], axis=0)

    with jax.named_scope("gather"):
        for m in range(0, MODES, 2):
            pair = [spread[pl.ds(m + i, SECTORS, stride=HROWS), :] for i in range(2)]
            both = twice(jnp.concatenate(pair, axis=1))
            result = jnp.dot(split_ref[...], both, preferred_element_type=F32)
            for i in range(2):
                gather[pl.ds(m + i, SECTORS, stride=MODES), :] = result[:, LANES * i:LANES * (i + 1)]
        counts = spread[pl.ds(MODES, SECTORS, stride=HROWS), :]
        power[...] = jnp.dot(square_ref[...], twice(counts), preferred_element_type=F32)

        def split_step(j, c):
            g = gather[pl.ds(pl.multiple_of(j * LANES, LANES), LANES), :]
            high = g.astype(BF16)
            gather_split[j] = jnp.concatenate([high, (g - high.astype(F32)).astype(BF16)], axis=1)
            return c

        lax.fori_loop(0, SEC, split_step, 0, unroll=2)
        tip_power_ref[...] = jnp.broadcast_to(jnp.sum(tip_sum, axis=1, keepdims=True), (MODES, LANES))


    with jax.named_scope("transform1"):
        transform(1)
    send_out(1, 1, 30)

    lane_ids = lax.broadcasted_iota(jnp.int32, (FAM, LANES), 1)

    def project_step(j, mode_power):
        rows = jnp.concatenate([mid[h, 2 * j + l] for l in range(2) for h in range(CHUNKS)], axis=0)
        both = lax.dot_general(
            jnp.concatenate([rows, rows], axis=1), gather_split[j], NT, preferred_element_type=F32
        )
        pair = jnp.where(lane_ids < MODES, both[:FAM], both[FAM:])
        part[:, j] = pair.reshape(DOFS, QF, LANES)
        rows = rows.astype(F32)
        for l in range(2):
            one = rows[FAM * l:FAM * (l + 1)]
            share = jnp.sum(one * one * power[pl.ds(2 * j + l, 1), :], axis=1, keepdims=True)
            mode_power = jnp.where(lane_ids == SEC * l + j, share, mode_power)
        return mode_power

    with jax.named_scope("project"):
        mode_power = lax.fori_loop(0, SEC, project_step, jnp.zeros((FAM, LANES), F32), unroll=4)
        part[:, SEC] = mode_power.reshape(DOFS, QF, LANES)
        part[:, SEC + 1] = jnp.zeros((DOFS, QF, LANES), F32)

    to_core[...] = part[pl.ds(2 * (1 - core), 2)].reshape(2, PAIRS, 2 * QF, LANES).astype(BF16)
    push("core", to_core, from_core, me, q ^ 1)
    arrived("core", from_core)
    sums = part[pl.ds(2 * core, 2)] + from_core[...].astype(F32).reshape(2, 2 * PAIRS, QF, LANES)
    half[...] = sums.reshape(2 * 2 * PAIRS * QF, LANES)

    lane = lax.broadcasted_iota(jnp.int32, (8, LANES), 1)
    row = lax.broadcasted_iota(jnp.int32, (8, LANES), 0)
    family_row = lax.broadcasted_iota(jnp.int32, (QF, FAM), 0)
    family_lane = lax.broadcasted_iota(jnp.int32, (QF, FAM), 1)
    with jax.named_scope("turn"):
        for i in range(2):
            at = 2 * PAIRS * QF * i
            turned = []
            for f in range(QF):
                one = half[pl.ds(at + f, SEC, stride=QF), :].T
                one = jnp.concatenate([one[:MODES], one[MODES:]], axis=1)
                turned.append(one.reshape(NXY, 8, LANES))
            for f in range(0, QF, 2):
                mine_xy[NXY * i:NXY * (i + 1), f // 2] = jnp.concatenate(turned[f:f + 2], axis=1).astype(BF16)
            nominal = jnp.zeros((QF, LANES), F32)
            for l in range(2):
                own = jnp.where(
                    family_row + QF * (2 * core + i) == family_lane, nominal_ref[pl.ds(l, 1), :], 0.0
                )
                own = jnp.sum(own, axis=1, keepdims=True)
                nominal = jnp.where((lane == SEC * l + me) & (lo == i), own, nominal)
            high = nominal.astype(BF16)
            rest = nominal - high.astype(F32)
            middle = rest.astype(BF16)
            last = (rest - middle.astype(F32)).astype(BF16)
            power_tile = half[pl.ds(at + SEC * QF, QF), :].astype(BF16)
            for k in range(NXY):
                mine_xy[NXY * i + k, 4] = jnp.concatenate([power_tile, high], axis=0)
                mine_xy[NXY * i + k, 5] = jnp.concatenate([middle, last], axis=0)
    slot = NXY * lo + xy
    for b in range(2):
        for k in range(1 - b, NXY):
            push("xy", mine_xy.at[NXY * (lo ^ b) + (xy ^ k)], from_xy.at[slot], me ^ k, q ^ (2 * b))
    send_out(1, 30, 42)
    from_xy[slot] = mine_xy[slot]
    arrived("xy", from_xy.at[pl.ds(0, 2 * NXY - 1)])
    column = jnp.sum(from_xy[...].astype(F32), axis=0)
    families = column[:4].reshape(QF, 8, LANES)
    power_tile, nominal = column[4, :8], column[4, 8:] + column[5, :8] + column[5, 8:]
    mine_z[:, 0] = families
    for i in range(NZ):
        mine_z[i, 1] = power_tile
        mine_z[i, 2] = nominal
    for k in range(1, NZ):
        push("z", mine_z.at[z ^ k], from_z.at[z], me ^ (NXY * k), q)
    send_out(1, 42, 54)
    from_z[z] = mine_z[z]
    arrived("z", from_z.at[pl.ds(0, NZ - 1)])
    whole = jnp.sum(from_z[...], axis=0)

    with jax.named_scope("normal"):
        projection = whole[0]
        mode_power, nominal = (
            jnp.sum(jnp.where(row == z, whole[i], 0.0), axis=0, keepdims=True) for i in (1, 2)
        )
        tip_power = tip_power_ref[pl.ds(pl.multiple_of(8 * xy, 8), 8), :]
        mac = (SECTORS * TIPS) * projection * projection / ((mode_power + 1e-06) * (tip_power + 1e-06))
        own_mode = lax.broadcasted_iota(jnp.int32, (8, MODES), 1) == 8 * xy + lax.broadcasted_iota(
            jnp.int32, (8, MODES), 0
        )
        pairing = jnp.sum(jnp.where(own_mode, pairing_ref[...].astype(F32), 0.0), axis=1, keepdims=True)
        measured = jnp.sum(jnp.where(own_mode, measured_ref[...], 0.0), axis=1, keepdims=True)
        family = (QF * quarter + z).astype(F32)
        weight = mac + jnp.where(pairing == family, 4.0, 0.0)
        pull = weight * ((measured - nominal) * projection)
        mac_rows = lax.dot_general(
            mac, jnp.where(own_mode, 1.0, 0.0), (((0,), (0,)), ((), ())),
            precision=HIGHEST, preferred_element_type=F32,
        )

        forth, back = forth_ref[...], back_ref[...]
        amps = jnp.dot(projection, forth, precision=HIGHEST, preferred_element_type=F32)
        amps_column = lax.dot_general(back, projection, NT, precision=HIGHEST, preferred_element_type=F32)
        left = jnp.concatenate([back * weight[k:k + 1, :] for k in range(8)], axis=0)
        pairs = jnp.dot(left, forth, precision=HIGHEST, preferred_element_type=F32)
        normal = jnp.zeros((SECTORS, SECTORS), F32)
        for k in range(8):
            normal += amps_column[:, k:k + 1] * (amps[k:k + 1, :] * pairs[SECTORS * k:SECTORS * (k + 1)])
        pulled = jnp.dot(pull, forth, precision=HIGHEST, preferred_element_type=F32)
        rhs = jnp.sum(amps * pulled, axis=0, keepdims=True)
        factor = 1.0 / (FAM * MODES * TIPS)
        normal = normal * factor
        rows = (
            normal[:SEC], normal[SEC:], jnp.broadcast_to(rhs * factor, (SEC, SECTORS)),
            jnp.concatenate([mac_rows[:SEC], mac_rows[SEC:]], axis=1),
        )
        for i in range(4):
            mine_sec[:, :, i, :] = rows[i].reshape(NZ, NXY, SECTORS)

    for k in range(1, NXY):
        push("rows_xy", mine_sec.at[:, xy ^ k], from_sec.at[xy], me ^ k, q)
    send_out(1, 54, SEC)
    from_sec[xy] = mine_sec[:, xy]
    arrived("rows_xy", from_sec.at[pl.ds(0, NXY - 1)])
    mine_rows[...] = jnp.sum(from_sec[...], axis=0)
    slot = NZ * q + z
    for b in range(DOFS):
        for k in range(0 if b else 1, NZ):
            push("rows", mine_rows.at[z ^ k], from_rows.at[slot], me ^ (NXY * k), q ^ b)
    from_rows[slot] = mine_rows[z]
    arrived("rows", from_rows.at[pl.ds(0, DOFS * NZ - 1)])
    rows = jnp.sum(from_rows[...], axis=0)
    normal_ref[...] = rows[:2]
    pair_lane = lax.broadcasted_iota(jnp.int32, (1, 2), 1)
    rhs_lane = lax.broadcasted_iota(jnp.int32, (1, LANES), 1)
    ends = [
        jnp.sum(jnp.where(rhs_lane == 2 * me + l, rows[2:3], 0.0), axis=1, keepdims=True) for l in range(2)
    ]
    rhs_ref[...] = jnp.where(pair_lane == 0, ends[0], ends[1])
    for i in range(DOFS):
        tile = from_rows[NZ * i:NZ * (i + 1), 3, :]
        for l in range(2):
            mac_ref[l, pl.ds(QF * (2 * (i % 2) + i // 2), QF), :] = tile[:, MODES * l:MODES * (l + 1)]

    for h in range(CHUNKS):
        arrived(f"out{h}", out_ref.at[:, pl.ds(ROWS * h, ROWS), pl.ds(0, LANES * (SEC - 1))])
        own = out_ref.at[:, pl.ds(ROWS * h, ROWS), pl.ds(0, LANES)]
        local(f"out{h}", own, own).wait()
    for stage, ref in sent:
        total(stage, ref).wait_send()


def write(*refs):
    count = len(refs) // 2
    copies = [pltpu.make_async_copy(refs[i], refs[count + i], refs[-1].at[i]) for i in range(count)]
    for copy in copies:
        copy.start()
    for copy in copies:
        copy.wait()


def on_device(sector_modes, tip_modes, tip_index, nominal_eig, measured_eig, pairing):
    constants = [jnp.asarray(a) for a in tables()]
    vmem = pl.BlockSpec(memory_space=pltpu.VMEM)
    hbm = pl.BlockSpec(memory_space=pltpu.HBM)
    tile = (QF, LANES)
    results = pl.pallas_call(
        body,
        out_shape=(
            jax.ShapeDtypeStruct(sector_modes.shape, BF16),
            jax.ShapeDtypeStruct((2, FAM, MODES), F32),
            jax.ShapeDtypeStruct((2, SECTORS), F32),
            jax.ShapeDtypeStruct((1, 2), F32),
        ),
        in_specs=[hbm] * 11,
        out_specs=(pl.BlockSpec(memory_space=pl.ANY), vmem, vmem, vmem),
        scratch_shapes=[
            pltpu.VMEM((SECTORS, TIPS), jnp.int32),
            pltpu.VMEM((2, FAM), F32),
            pltpu.VMEM((1, MODES), F32),
            pltpu.VMEM((1, MODES), jnp.int32),
            pltpu.VMEM((SECTORS, SECTORS), BF16),
            pltpu.VMEM((SECTORS, 2 * SECTORS), BF16),
            pltpu.VMEM((SECTORS, 2 * SECTORS), BF16),
            pltpu.VMEM((SECTORS, SECTORS), F32),
            pltpu.VMEM((SECTORS, SECTORS), F32),
            pltpu.VMEM((CHUNKS, SECTORS, ROWS, LANES), BF16),
            pltpu.VMEM((SECTORS * ROWS, LANES), F32),
            pltpu.VMEM((SECTORS * ROWS, LANES), F32),
            pltpu.VMEM((CHUNKS, SECTORS, ROWS, LANES), BF16),
            pltpu.VMEM((2, NZ, NX, 2 * NY, MODES // 2, TIPS), BF16),
            pltpu.VMEM((SECTORS * HROWS, LANES), F32),
            pltpu.VMEM((SECTORS * MODES, LANES), F32),
            pltpu.VMEM((SEC, LANES, 2 * LANES), BF16),
            pltpu.VMEM((SECTORS, LANES), F32),
            pltpu.VMEM((MODES, LANES), F32),
            pltpu.VMEM((DOFS, 2 * PAIRS) + tile, F32),
            pltpu.VMEM((2, PAIRS, 2 * QF, LANES), BF16),
            pltpu.VMEM((2, PAIRS, 2 * QF, LANES), BF16),
            pltpu.VMEM((2 * 2 * PAIRS * QF, LANES), F32),
            pltpu.VMEM((2 * NXY, 6, 16, LANES), BF16),
            pltpu.VMEM((2 * NXY, 6, 16, LANES), BF16),
            pltpu.VMEM((NZ, 3) + tile, F32),
            pltpu.VMEM((NZ, 3) + tile, F32),
            pltpu.VMEM((NZ, NXY, 4, LANES), F32),
            pltpu.VMEM((NXY, NZ, 4, LANES), F32),
            pltpu.VMEM((NZ, 4, LANES), F32),
            pltpu.VMEM((DOFS * NZ, 4, LANES), F32),
            pltpu.SemaphoreType.DMA((len(STAGES),)),
            pltpu.SemaphoreType.DMA((len(STAGES),)),
            pltpu.SemaphoreType.DMA((len(LOCAL),)),
        ],
        compiler_params=pltpu.CompilerParams(
            collective_id=0, has_side_effects=True, vmem_limit_bytes=40 * 2**20
        ),
        name="identify",
    )(
        *[
            pltpu.with_memory_space_constraint(a, pltpu.HBM)
            for a in (
                sector_modes, tip_modes, tip_index, nominal_eig, measured_eig.reshape(1, MODES),
                pairing.reshape(1, MODES), *constants,
            )
        ]
    )
    harmonic, mac, normal, rhs = pl.pallas_call(
        write,
        out_shape=[jax.ShapeDtypeStruct(a.shape, a.dtype) for a in results],
        in_specs=[vmem] * 4,
        out_specs=[hbm] * 4,
        scratch_shapes=[
            pltpu.SemaphoreType.DMA((4,)),
        ],
        name="write",
    )(*[pltpu.with_memory_space_constraint(a, pltpu.VMEM) for a in results])
    return harmonic, mac, normal, rhs.reshape(2)


def solution(mesh):
    return jax.shard_map(
        on_device,
        mesh=mesh,
        in_specs=(P("sec", None, "dof"), P("sec", None, None), P(), P("sec", None), P(), P()),
        out_specs=(P("sec", None, "dof"), P("sec", None, None), P("sec", None), P("sec")),
        check_vma=False,
    )
```
